512 devices in a mesh: row: 32 (over y, x), col: 16 (over z, core).
Axes of the slice: x: 4, y: 8, z: 8, core: 2. Of those that a mesh axis runs over, the one named last changes fastest.
Arguments:
- points: float32 [8, 65536], P(None, ('row', 'col')), may hold values from -1.8 to 1.8
- inverse_scale: float32 [8], replicated, may hold values from 0.5 to 1
- targets: float32 [16, 65536], P(None, ('row', 'col')), may hold values from -3.5 to 5.5
- noise_var: float32 [16], replicated, may hold values from 0.5 to 2
Outputs:
- solution: float32 [16, 65536], P(None, ('row', 'col'))
- residual: float32 [16, 65536], P(None, ('row', 'col'))
The draws below stay inside these ranges and needn't reach their ends.
All inputs are finite; a program needn't handle non-finite values.
Results may differ from the reference program's by a relative error of at most 0.0015.
Values sent between devices are 32-bit elements; how exact they have to be, the bound alone decides.
No kernel may reach another device: no remote copies, remote signals or barrier semaphores. Data moves between devices by JAX's collectives and lax.ppermute only.
A program may use at most 64 MiB of HBM per device.

```python
import math
import jax
import jax.numpy as jnp
from jax import lax

NFEAT = 8
NRHS = 16
ITERS = 2
NPTS = 65536


def draw_targets(key, part):
    key = jax.random.fold_in(key, 7)
    offset_key, noise_key = jax.random.split(key)
    offset = jax.random.uniform(offset_key, (NRHS, 1), jnp.float32, 0.5, 1.5)
    noise = jax.random.truncated_normal(noise_key, -4.0, 4.0, (NRHS, NPTS), jnp.float32)
    return (offset + noise).astype(jnp.float32)


def block_levels(key, dims, pieces, low, high):
    gain, own = 1.0, jax.random.fold_in(key, 6)
    for dim, shards_of in pieces:
        steps = jnp.exp(jax.random.uniform(jax.random.fold_in(own, dim), (shards_of,), jnp.float32, low / len(pieces), high / len(pieces)))
        gain = gain * jnp.repeat(steps, dims[dim] // shards_of).reshape([-1 if axis == dim else 1 for axis in range(len(dims))])
    return gain


def setup_inputs(seed: int = 0) -> dict:
    seeds = jax.random.split(jax.random.key(seed), 5)
    return {
        "points": jnp.clip(jax.random.uniform(seeds[0], (NFEAT, NPTS), jnp.float32, -1.8, 1.8) * block_levels(seeds[0], (NFEAT, NPTS), ((1, 512),), -0.4, 0.0), -1.8, 1.8),
        "inverse_scale": jnp.clip(jnp.exp(jax.random.uniform(seeds[1], (NFEAT,), jnp.float32, math.log(0.5), math.log(1.0))), 0.5, 1.0),
        "targets": draw_targets(jax.random.fold_in(seeds[4], 71), 0),
        "noise_var": jnp.clip(jnp.exp(jax.random.uniform(seeds[3], (NRHS,), jnp.float32, math.log(0.5), math.log(2.0))), 0.5, 2.0),
    }


exact_mode = lax.Precision.HIGHEST


def kernel_apply(scaled, vector):
    column_count = scaled.shape[1]
    block_cols = math.gcd(column_count, 1024)
    block_count = column_count // block_cols
    half_norms = 0.5 * jnp.sum(scaled * scaled, axis=0)

    def advance(accumulated, block_index):
        offset = (block_index * block_cols).astype(jnp.int32)
        col_z = lax.dynamic_slice_in_dim(scaled, offset, block_cols, 1)
        col_v = lax.dynamic_slice_in_dim(vector, offset, block_cols, 1)
        col_half = 0.5 * jnp.sum(col_z * col_z, axis=0)
        inner_products = jnp.einsum("fb,fr->br", col_z, scaled, precision=exact_mode)
        kernel = jnp.exp(inner_products - col_half[:, None] - half_norms[None, :])
        return accumulated + jnp.dot(col_v, kernel, precision=exact_mode, preferred_element_type=jnp.float32), None

    initial = jnp.zeros(vector.shape, jnp.float32)
    accumulated, unused = lax.scan(advance, initial, jnp.arange(block_count, dtype=jnp.int32))
    return accumulated


def reference(points, inverse_scale, targets, noise_var):
    scaled = points * inverse_scale[:, None]
    solution = jnp.zeros_like(targets)
    residual = targets
    direction = targets
    norm_now = jnp.sum(residual * residual, axis=1)
    for turn in range(ITERS):
        image = kernel_apply(scaled, direction) + noise_var[:, None] * direction
        step_size = norm_now / jnp.sum(direction * image, axis=1)
        solution = solution + step_size[:, None] * direction
        residual = residual - step_size[:, None] * image
        norm_next = jnp.sum(residual * residual, axis=1)
        direction = residual + (norm_next / norm_now)[:, None] * direction
        norm_now = norm_next
    return solution, residual
```

```python
import functools
import math

import jax
import jax.numpy as jnp
from jax import lax
from jax.experimental import pallas as pl
from jax.experimental.pallas import tpu as pltpu
from jax.sharding import PartitionSpec as P

LANES = 128
NFEAT = 8
NRHS = 16
FEATURE_ROWS = 64
ROOT_LOG2E = math.sqrt(math.log2(math.e))
STEP = 512
WIDE = 256


def pieces(value):
    high = value.astype(jnp.bfloat16).astype(jnp.float32)
    rest = value - high
    middle = rest.astype(jnp.bfloat16).astype(jnp.float32)
    low = (rest - middle).astype(jnp.bfloat16).astype(jnp.float32)
    return high, middle, low


def features(scaled, is_left):
    z = scaled * ROOT_LOG2E
    high, middle, low = pieces(z)
    norm_pieces = pieces(-0.5 * jnp.sum(z * z, axis=0, keepdims=True))
    row = lax.broadcasted_iota(jnp.int32, z.shape, 0)
    start = 0 if is_left else 3
    norms = jnp.where((row < 6) & ((row < start) | (row >= start + 3)), 1.0, 0.0)
    for place, piece in enumerate(norm_pieces):
        norms = jnp.where(row == start + place, piece, norms)
    if is_left:
        parts = [high, high, middle, middle, high, low]
    else:
        parts = [high, middle, high, middle, low, high]
    return jnp.concatenate(parts + [norms, jnp.zeros_like(z)], axis=0)


def dot(left, right):
    return lax.dot_general(left, right, (((1,), (0,)), ((), ())), preferred_element_type=jnp.float32)


def image_kernel(left_ref, vector_ref, right_ref, out_ref, left, right, vector, total):
    for block in range(right_ref.shape[0]):
        span = pl.ds(block * LANES, LANES)
        right[:, span] = features(right_ref[block], False).astype(jnp.bfloat16)
    for block in range(left_ref.shape[0]):
        span = pl.ds(block * LANES, LANES)
        left[span, :] = features(left_ref[block, :NFEAT, :], True).T.astype(jnp.bfloat16)
        vector[:, span] = jnp.concatenate(pieces(vector_ref[block]), axis=0).astype(jnp.bfloat16)
    total[...] = jnp.zeros_like(total)

    def advance(step, unused):
        offset = pl.multiple_of(step * STEP, STEP)
        left_block = left[pl.ds(offset, STEP), :]
        vector_block = vector[:, pl.ds(offset, STEP)]
        for place in range(right.shape[1] // WIDE):
            span = pl.ds(place * WIDE, WIDE)
            kernel = jnp.exp2(dot(left_block, right[:, span]))
            high = kernel.astype(jnp.bfloat16)
            low = (kernel - high.astype(jnp.float32)).astype(jnp.bfloat16)
            total[:, span] += dot(vector_block, high) + dot(vector_block, low)
        return unused

    lax.fori_loop(0, left.shape[0] // STEP, advance, 0)
    for block in range(right_ref.shape[0]):
        terms = total[:, pl.ds(block * LANES, LANES)]
        out_ref[block] = terms[:NRHS] + terms[NRHS : 2 * NRHS] + terms[2 * NRHS :]


def image_terms(left, vector, right):
    left_count, right_count = left.shape[0] * LANES, right.shape[0] * LANES
    vmem = pl.BlockSpec(memory_space=pltpu.VMEM)
    return pl.pallas_call(
        image_kernel,
        out_shape=jax.ShapeDtypeStruct((right.shape[0], NRHS, LANES), jnp.float32),
        in_specs=[vmem] * 3,
        out_specs=vmem,
        scratch_shapes=[
            pltpu.VMEM((left_count, FEATURE_ROWS), jnp.bfloat16),
            pltpu.VMEM((FEATURE_ROWS, right_count), jnp.bfloat16),
            pltpu.VMEM((3 * NRHS, left_count), jnp.bfloat16),
            pltpu.VMEM((3 * NRHS, right_count), jnp.float32),
        ],
        compiler_params=pltpu.CompilerParams(vmem_limit_bytes=40 << 20),
    )(left, vector, right)


def exchange(blocks, axis):
    return lax.all_to_all(blocks, axis, 0, 0, tiled=True)


def gather(block, axis, count):
    return exchange(jnp.broadcast_to(block[None], (count,) + block.shape), axis)


def tile_of(sums):
    stacked = jnp.stack(sums)
    return jnp.pad(stacked, ((0, 8 - stacked.shape[0]), (0, LANES - NRHS)))


def inner(left, right):
    return jnp.sum(left * right, axis=1)


def on_device(rows, cols, points, inverse_scale, targets, noise_var):
    scaled = points * inverse_scale[:, None]
    noise = noise_var[:, None]
    left = gather(jnp.concatenate([scaled, targets], axis=0), "row", rows)
    right = gather(scaled, "col", cols)

    partial = image_terms(left, left[:, NFEAT:], right)
    image = jnp.sum(exchange(partial, "col"), axis=0) + noise * targets

    sums = tile_of([inner(targets, targets), inner(targets, image)])
    gathered = gather(jnp.concatenate([image, sums], axis=0), "row", rows)
    partial = image_terms(left, gathered[:, :NRHS], right)
    sums = jnp.sum(gathered[:, NRHS:], axis=0)
    partial = jnp.concatenate([partial, jnp.broadcast_to(sums[None], (cols,) + sums.shape)], axis=1)
    reduced = jnp.sum(exchange(partial, "col"), axis=0)
    image_image = reduced[:NRHS] + noise * image

    norm_now, curvature = reduced[NRHS, :NRHS], reduced[NRHS + 1, :NRHS]
    step_size = (norm_now / curvature)[:, None]
    residual = targets - step_size * image
    residual_image = image - step_size * image_image
    sums = tile_of([inner(residual, residual), inner(residual, residual_image), inner(residual, image)])
    sums = jnp.sum(gather(sums, "col", cols), axis=0)
    sums = jnp.sum(gather(sums, "row", rows), axis=0)
    norm_next = sums[0, :NRHS]
    ratio = norm_next / norm_now
    next_curvature = sums[1, :NRHS] + ratio * (2.0 * sums[2, :NRHS] + ratio * curvature)
    next_step = (norm_next / next_curvature)[:, None]
    ratio = ratio[:, None]
    solution = step_size * targets + next_step * (residual + ratio * targets)
    residual = residual - next_step * (residual_image + ratio * image)
    return (solution, residual)


def solution(mesh):
    return jax.shard_map(
        functools.partial(on_device, mesh.shape["row"], mesh.shape["col"]),
        mesh=mesh,
        in_specs=(P(None, ("row", "col")), P(), P(None, ("row", "col")), P()),
        out_specs=(P(None, ("row", "col")), P(None, ("row", "col"))),
        check_vma=False,
    )
```

```python
import functools
import math

import jax
import jax.numpy as jnp
from jax import lax
from jax.experimental import pallas as pl
from jax.experimental.pallas import tpu as pltpu
from jax.sharding import PartitionSpec as P

LANES = 128
NFEAT = 8
NRHS = 16
SUMS = 8
FEATURE_ROWS = 64
ROOT_LOG2E = math.sqrt(math.log2(math.e))
STEP = 512
WIDE = 256


def pieces(value):
    high = value.astype(jnp.bfloat16).astype(jnp.float32)
    rest = value - high
    middle = rest.astype(jnp.bfloat16).astype(jnp.float32)
    low = (rest - middle).astype(jnp.bfloat16).astype(jnp.float32)
    return high, middle, low


def features(scaled, is_left):
    z = scaled * ROOT_LOG2E
    high, middle, low = pieces(z)
    norm_pieces = pieces(-0.5 * jnp.sum(z * z, axis=0, keepdims=True))
    row = lax.broadcasted_iota(jnp.int32, z.shape, 0)
    start = 0 if is_left else 3
    norms = jnp.where((row < 6) & ((row < start) | (row >= start + 3)), 1.0, 0.0)
    for place, piece in enumerate(norm_pieces):
        norms = jnp.where(row == start + place, piece, norms)
    if is_left:
        parts = [high, high, middle, middle, high, low]
    else:
        parts = [high, middle, high, middle, low, high]
    return jnp.concatenate(parts + [norms, jnp.zeros_like(z)], axis=0)


def dot(left, right):
    return lax.dot_general(left, right, (((1,), (0,)), ((), ())), preferred_element_type=jnp.float32)


def write_features(left_ref, right_ref, left, right):
    for block in range(right_ref.shape[0]):
        span = pl.ds(block * LANES, LANES)
        right[:, span] = features(right_ref[block, :NFEAT, :], False).astype(jnp.bfloat16)
    for block in range(left_ref.shape[0]):
        span = pl.ds(block * LANES, LANES)
        left[span, :] = features(left_ref[block, :NFEAT, :], True).T.astype(jnp.bfloat16)


def write_vector(block, value, vector):
    span = pl.ds(block * LANES, LANES)
    vector[:, span] = jnp.concatenate(pieces(value), axis=0).astype(jnp.bfloat16)


def multiply(left, right, vector, total):
    total[...] = jnp.zeros_like(total)

    def advance(step, unused):
        offset = pl.multiple_of(step * STEP, STEP)
        left_block = left[pl.ds(offset, STEP), :]
        vector_block = vector[:, pl.ds(offset, STEP)]
        for place in range(right.shape[1] // WIDE):
            span = pl.ds(place * WIDE, WIDE)
            kernel = jnp.exp2(dot(left_block, right[:, span]))
            high = kernel.astype(jnp.bfloat16)
            low = (kernel - high.astype(jnp.float32)).astype(jnp.bfloat16)
            total[:, span] += dot(vector_block, high) + dot(vector_block, low)
        return unused

    lax.fori_loop(0, left.shape[0] // STEP, advance, 0)


def block_terms(total, block):
    terms = total[:, pl.ds(block * LANES, LANES)]
    return terms[:NRHS] + terms[NRHS : 2 * NRHS] + terms[2 * NRHS :]


def write_sums(products, out_ref):
    empty = jnp.zeros((LANES - NRHS * len(products), LANES), jnp.float32)
    turned = jnp.concatenate(products + [empty], axis=0).T
    row = jnp.sum(turned, axis=0, keepdims=True)
    for block in range(out_ref.shape[0]):
        out_ref[block, NRHS:, :] = jnp.broadcast_to(row, (SUMS, LANES))


def first_kernel(left_ref, right_ref, out_ref, left, right, vector, total):
    write_features(left_ref, right_ref, left, right)
    square = jnp.zeros((NRHS, LANES), jnp.float32)
    for block in range(left_ref.shape[0]):
        value = left_ref[block, NFEAT:, :]
        write_vector(block, value, vector)
        square += value * value
    multiply(left, right, vector, total)
    product = jnp.zeros((NRHS, LANES), jnp.float32)
    for block in range(right_ref.shape[0]):
        terms = block_terms(total, block)
        out_ref[block, :NRHS, :] = terms
        product += terms * right_ref[block, NFEAT:, :]
    write_sums([product, square], out_ref)


def second_kernel(
    left_ref, right_ref, left_image_ref, right_image_ref, noise_ref, out_ref, left, right, vector, total
):
    row = jnp.zeros((SUMS, LANES), jnp.float32)
    for block in range(left_ref.shape[0]):
        row += left_image_ref[block, NRHS:, :]
    product = jnp.broadcast_to(row[:1], (LANES, LANES)).T[:NRHS]
    norm = jnp.broadcast_to(left_image_ref[0, NRHS : NRHS + 1, :], (LANES, LANES)).T[NRHS : 2 * NRHS]
    step_size = norm / (product + noise_ref[...] * norm)

    write_features(left_ref, right_ref, left, right)
    square = jnp.zeros((NRHS, LANES), jnp.float32)
    crossed = jnp.zeros((NRHS, LANES), jnp.float32)
    for block in range(left_ref.shape[0]):
        image = left_image_ref[block, :NRHS, :]
        residual = left_ref[block, NFEAT:, :] - step_size * image
        write_vector(block, residual, vector)
        square += residual * residual
        crossed += residual * image
    multiply(left, right, vector, total)
    product = jnp.zeros((NRHS, LANES), jnp.float32)
    for block in range(right_ref.shape[0]):
        terms = block_terms(total, block)
        out_ref[block, :NRHS, :] = terms
        product += terms * (right_ref[block, NFEAT:, :] - step_size * right_image_ref[block])
    write_sums([product, square, crossed], out_ref)


def call_kernel(body, left, right, *others):
    left_count, right_count = left.shape[0] * LANES, right.shape[0] * LANES
    vmem = pl.BlockSpec(memory_space=pltpu.VMEM)
    return pl.pallas_call(
        body,
        out_shape=jax.ShapeDtypeStruct((right.shape[0], NRHS + SUMS, LANES), jnp.float32),
        in_specs=[vmem] * (2 + len(others)),
        out_specs=vmem,
        scratch_shapes=[
            pltpu.VMEM((left_count, FEATURE_ROWS), jnp.bfloat16),
            pltpu.VMEM((FEATURE_ROWS, right_count), jnp.bfloat16),
            pltpu.VMEM((3 * NRHS, left_count), jnp.bfloat16),
            pltpu.VMEM((3 * NRHS, right_count), jnp.float32),
        ],
        compiler_params=pltpu.CompilerParams(vmem_limit_bytes=40 << 20),
    )(left, right, *others)


def exchange(blocks, axis):
    return lax.all_to_all(blocks, axis, 0, 0, tiled=True)


def gather(block, axis, count):
    return exchange(jnp.broadcast_to(block[None], (count,) + block.shape), axis)


def on_device(rows, points, inverse_scale, targets, noise_var):
    noise = noise_var[:, None]
    known = jnp.concatenate([points * inverse_scale[:, None], targets], axis=0)
    left = gather(known, "row", rows)
    right = lax.all_gather(known, "col", axis=0)

    reduced = jnp.sum(exchange(call_kernel(first_kernel, left, right), "col"), axis=0)
    image = reduced[:NRHS] + noise * targets
    norm_now = reduced[NRHS, NRHS : 2 * NRHS]

    left_image = gather(jnp.concatenate([image, reduced[NRHS:]], axis=0), "row", rows)
    right_image = lax.all_gather(image, "col", axis=0)
    wide_noise = jnp.broadcast_to(noise, (NRHS, LANES))
    partial = call_kernel(second_kernel, left, right, left_image, right_image, wide_noise)
    curvature = jnp.sum(left_image[:, NRHS, :NRHS], axis=0) + noise_var * norm_now
    step_size = (norm_now / curvature)[:, None]
    residual = targets - step_size * image

    reduced = jnp.sum(exchange(partial, "col"), axis=0)
    norm_next = reduced[NRHS, NRHS : 2 * NRHS]
    crossed = reduced[NRHS, 2 * NRHS : 3 * NRHS]
    sums = gather(reduced[NRHS:], "row", rows)
    residual_curvature = jnp.sum(sums[:, 0, :NRHS], axis=0) + noise_var * norm_next
    ratio = norm_next / norm_now
    next_curvature = residual_curvature + ratio * (2.0 * crossed + ratio * curvature)
    next_step = (norm_next / next_curvature)[:, None]
    ratio = ratio[:, None]
    residual_image = reduced[:NRHS] + noise * residual
    solution = step_size * targets + next_step * (residual + ratio * targets)
    residual = residual - next_step * (residual_image + ratio * image)
    return (solution, residual)


def solution(mesh):
    return jax.shard_map(
        functools.partial(on_device, mesh.shape["row"]),
        mesh=mesh,
        in_specs=(P(None, ("row", "col")), P(), P(None, ("row", "col")), P()),
        out_specs=(P(None, ("row", "col")), P(None, ("row", "col"))),
        check_vma=False,
    )
```

```python
import functools
import math

import jax
import jax.numpy as jnp
from jax import lax
from jax.experimental import pallas as pl
from jax.experimental.pallas import tpu as pltpu
from jax.sharding import PartitionSpec as P

LANES = 128
NFEAT = 8
NRHS = 16
SUMS = 8
FEATURE_ROWS = 64
ROOT_LOG2E = math.sqrt(math.log2(math.e))
STEP = 512
WIDE = 256
VMEM_LIMIT = 16 << 20


def pieces(value):
    high = value.astype(jnp.bfloat16).astype(jnp.float32)
    rest = value - high
    middle = rest.astype(jnp.bfloat16).astype(jnp.float32)
    low = (rest - middle).astype(jnp.bfloat16).astype(jnp.float32)
    return high, middle, low


def features(scaled, is_left):
    z = scaled * ROOT_LOG2E
    high, middle, low = pieces(z)
    norm_pieces = pieces(-0.5 * jnp.sum(z * z, axis=0, keepdims=True))
    row = lax.broadcasted_iota(jnp.int32, z.shape, 0)
    start = 0 if is_left else 3
    norms = jnp.where((row < 6) & ((row < start) | (row >= start + 3)), 1.0, 0.0)
    for place, piece in enumerate(norm_pieces):
        norms = jnp.where(row == start + place, piece, norms)
    if is_left:
        parts = [high, high, middle, middle, high, low]
    else:
        parts = [high, middle, high, middle, low, high]
    return jnp.concatenate(parts + [norms, jnp.zeros_like(z)], axis=0)


def dot(left, right):
    return lax.dot_general(left, right, (((1,), (0,)), ((), ())), preferred_element_type=jnp.float32)


def split_vector(value_of, vector):
    for block in range(vector.shape[1] // LANES):
        span = pl.ds(block * LANES, LANES)
        vector[:, span] = jnp.concatenate(pieces(value_of(block)), axis=0).astype(jnp.bfloat16)


def write_terms(total, out_ref):
    for block in range(out_ref.shape[0]):
        terms = total[:, pl.ds(block * LANES, LANES)]
        out_ref[block, :NRHS, :] = terms[:NRHS] + terms[NRHS : 2 * NRHS] + terms[2 * NRHS :]


def first_kernel(left_ref, right_ref, out_ref, high_ref, low_ref, left, right, vector, total):
    for block in range(right_ref.shape[0]):
        span = pl.ds(block * LANES, LANES)
        right[:, span] = features(right_ref[block], False).astype(jnp.bfloat16)
    for block in range(left_ref.shape[0]):
        span = pl.ds(block * LANES, LANES)
        left[span, :] = features(left_ref[block, :NFEAT, :], True).T.astype(jnp.bfloat16)
    split_vector(lambda block: left_ref[block, NFEAT:, :], vector)
    total[...] = jnp.zeros_like(total)

    def advance(step, unused):
        rows = pl.ds(pl.multiple_of(step * STEP, STEP), STEP)
        left_block = left[rows, :]
        vector_block = vector[:, rows]
        for place in range(right.shape[1] // WIDE):
            span = pl.ds(place * WIDE, WIDE)
            kernel = jnp.exp2(dot(left_block, right[:, span]))
            high = kernel.astype(jnp.bfloat16)
            low = (kernel - high.astype(jnp.float32)).astype(jnp.bfloat16)
            high_ref[rows, span] = high
            low_ref[rows, span] = low
            total[:, span] += dot(vector_block, high) + dot(vector_block, low)
        return unused

    lax.fori_loop(0, left.shape[0] // STEP, advance, 0)
    write_terms(total, out_ref)


def second_kernel(left_ref, image_ref, high_ref, low_ref, out_ref, vector, total):
    split_vector(lambda block: image_ref[block], vector)
    for place in range(total.shape[1] // WIDE):
        span = pl.ds(place * WIDE, WIDE)
        total[:, span] = dot(vector[...], high_ref[:, span]) + dot(vector[...], low_ref[:, span])
    write_terms(total, out_ref)
    square = jnp.zeros((NRHS, LANES), jnp.float32)
    product = jnp.zeros((NRHS, LANES), jnp.float32)
    for block in range(left_ref.shape[0]):
        target = left_ref[block, NFEAT:, :]
        square += target * target
        product += target * image_ref[block]
    empty = jnp.zeros((LANES - 2 * NRHS, LANES), jnp.float32)
    turned = jnp.concatenate([square, product, empty], axis=0).T
    row = jnp.sum(turned, axis=0, keepdims=True)
    for block in range(out_ref.shape[0]):
        out_ref[block, NRHS:, :] = jnp.broadcast_to(row, (SUMS, LANES))


VMEM_BLOCK = pl.BlockSpec(memory_space=pltpu.VMEM)


def first_product(left, right):
    left_count, right_count = left.shape[0] * LANES, right.shape[0] * LANES
    kept = pltpu.VMEM((left_count, right_count), jnp.bfloat16)
    return pl.pallas_call(
        first_kernel,
        out_shape=[jax.ShapeDtypeStruct((right.shape[0], NRHS, LANES), jnp.float32), kept, kept],
        in_specs=[VMEM_BLOCK] * 2,
        out_specs=[VMEM_BLOCK] * 3,
        scratch_shapes=[
            pltpu.VMEM((left_count, FEATURE_ROWS), jnp.bfloat16),
            pltpu.VMEM((FEATURE_ROWS, right_count), jnp.bfloat16),
            pltpu.VMEM((3 * NRHS, left_count), jnp.bfloat16),
            pltpu.VMEM((3 * NRHS, right_count), jnp.float32),
        ],
        compiler_params=pltpu.CompilerParams(vmem_limit_bytes=VMEM_LIMIT),
    )(left, right)


def second_product(left, image, high, low):
    left_count, right_count = high.shape
    return pl.pallas_call(
        second_kernel,
        out_shape=jax.ShapeDtypeStruct((right_count // LANES, NRHS + SUMS, LANES), jnp.float32),
        in_specs=[VMEM_BLOCK] * 4,
        out_specs=VMEM_BLOCK,
        scratch_shapes=[
            pltpu.VMEM((3 * NRHS, left_count), jnp.bfloat16),
            pltpu.VMEM((3 * NRHS, right_count), jnp.float32),
        ],
        compiler_params=pltpu.CompilerParams(vmem_limit_bytes=VMEM_LIMIT),
    )(left, image, high, low)


def exchange(blocks, axis):
    return lax.all_to_all(blocks, axis, 0, 0, tiled=True)


def gather(block, axis, count):
    return exchange(jnp.broadcast_to(block[None], (count,) + block.shape), axis)


def tile_of(sums):
    stacked = jnp.stack(sums)
    return jnp.pad(stacked, ((0, SUMS - stacked.shape[0]), (0, LANES - NRHS)))


def inner(left, right):
    return jnp.sum(left * right, axis=1)


def on_device(rows, cols, points, inverse_scale, targets, noise_var):
    noise = noise_var[:, None]
    scaled = points * inverse_scale[:, None]
    left = gather(jnp.concatenate([scaled, targets], axis=0), "row", rows)
    right = lax.all_gather(scaled, "col", axis=0)

    partial, high, low = first_product(left, right)
    image = jnp.sum(exchange(partial, "col"), axis=0) + noise * targets
    partial = second_product(left, gather(image, "row", rows), high, low)
    reduced = jnp.sum(exchange(partial, "col"), axis=0)
    image_image = reduced[:NRHS] + noise * image

    norm_now, curvature = reduced[NRHS, :NRHS], reduced[NRHS, NRHS : 2 * NRHS]
    step_size = (norm_now / curvature)[:, None]
    residual = targets - step_size * image
    residual_image = image - step_size * image_image
    sums = tile_of([inner(residual, residual), inner(residual, residual_image), inner(residual, image)])
    sums = jnp.sum(gather(sums, "col", cols), axis=0)
    sums = jnp.sum(gather(sums, "row", rows), axis=0)
    norm_next = sums[0, :NRHS]
    ratio = norm_next / norm_now
    next_curvature = sums[1, :NRHS] + ratio * (2.0 * sums[2, :NRHS] + ratio * curvature)
    next_step = (norm_next / next_curvature)[:, None]
    ratio = ratio[:, None]
    solution = step_size * targets + next_step * (residual + ratio * targets)
    residual = residual - next_step * (residual_image + ratio * image)
    return (solution, residual)


def solution(mesh):
    return jax.shard_map(
        functools.partial(on_device, mesh.shape["row"], mesh.shape["col"]),
        mesh=mesh,
        in_specs=(P(None, ("row", "col")), P(), P(None, ("row", "col")), P()),
        out_specs=(P(None, ("row", "col")), P(None, ("row", "col"))),
        check_vma=False,
    )
```

```python
import functools
import math

import jax
import jax.numpy as jnp
from jax import lax
from jax.experimental import pallas as pl
from jax.experimental.pallas import tpu as pltpu
from jax.sharding import PartitionSpec as P

LANES = 128
NFEAT = 8
NRHS = 16
SUMS = 8
FEATURE_ROWS = 64
ROOT_LOG2E = math.sqrt(math.log2(math.e))
STEP = 1024
WIDE = 256
KEPT = 3
VMEM_LIMIT = 40 << 20
SMALL_LIMIT = 4 << 20


def pieces(value):
    high = value.astype(jnp.bfloat16).astype(jnp.float32)
    rest = value - high
    middle = rest.astype(jnp.bfloat16).astype(jnp.float32)
    low = (rest - middle).astype(jnp.bfloat16).astype(jnp.float32)
    return high, middle, low


def features(scaled, is_left):
    z = scaled * ROOT_LOG2E
    high, middle, low = pieces(z)
    norm_pieces = pieces(-0.5 * jnp.sum(z * z, axis=0, keepdims=True))
    row = lax.broadcasted_iota(jnp.int32, z.shape, 0)
    start = 0 if is_left else 3
    norms = jnp.where((row < 6) & ((row < start) | (row >= start + 3)), 1.0, 0.0)
    for place, piece in enumerate(norm_pieces):
        norms = jnp.where(row == start + place, piece, norms)
    if is_left:
        parts = [high, high, middle, middle, high, low]
    else:
        parts = [high, middle, high, middle, low, high]
    return jnp.concatenate(parts + [norms, jnp.zeros_like(z)], axis=0)


def dot(left, right):
    return lax.dot_general(left, right, (((1,), (0,)), ((), ())), preferred_element_type=jnp.float32)


def split_vector(value_of, vector):
    for block in range(vector.shape[1] // LANES):
        span = pl.ds(block * LANES, LANES)
        vector[:, span] = jnp.concatenate(pieces(value_of(block))[:2], axis=0).astype(jnp.bfloat16)


def write_right(right_ref, right):
    for block in range(right_ref.shape[0]):
        span = pl.ds(block * LANES, LANES)
        right[:, span] = features(right_ref[block], False).astype(jnp.bfloat16)


def write_left(left_ref, left, begin):
    for block in range(begin, left_ref.shape[0]):
        span = pl.ds((block - begin) * LANES, LANES)
        left[span, :] = features(left_ref[block, :NFEAT, :], True).T.astype(jnp.bfloat16)


def write_terms(total, out_ref):
    for block in range(out_ref.shape[0]):
        terms = total[:, pl.ds(block * LANES, LANES)]
        out_ref[block, :NRHS, :] = terms[:NRHS] + terms[NRHS : 2 * NRHS] + terms[2 * NRHS :]


def spans(total):
    return [pl.ds(place * WIDE, WIDE) for place in range(total.shape[1] // WIDE)]


def add_terms(total, span, vector_block, high, low):
    total[: 2 * NRHS, span] += dot(vector_block, high)
    total[2 * NRHS :, span] += dot(vector_block[:NRHS], low)


def parts_of(left_block, right_block):
    kernel = jnp.exp2(dot(left_block, right_block))
    high = kernel.astype(jnp.bfloat16)
    return high, (kernel - high.astype(jnp.float32)).astype(jnp.bfloat16)


def rows_of(step):
    return pl.ds(pl.multiple_of(step * STEP, STEP), STEP)


def first_kernel(
    left_ref, right_ref, out_ref, high_ref, low_ref, left, right, vector, total, high_part, low_part, sent
):
    steps, kept = left.shape[0] // STEP, high_part.shape[0] // STEP
    write_right(right_ref, right)
    write_left(left_ref, left, 0)
    split_vector(lambda block: left_ref[block, NFEAT:, :], vector)
    total[...] = jnp.zeros_like(total)

    def copies(step):
        rows = rows_of(step)
        return [
            pltpu.make_async_copy(part.at[rows], ref.at[rows], sent.at[place, step])
            for place, (part, ref) in enumerate([(high_part, high_ref), (low_part, low_ref)])
        ]

    def advance(step, unused, keep):
        rows = rows_of(step)
        for span in spans(total):
            high, low = parts_of(left[rows, :], right[:, span])
            if keep:
                high_part[rows, span] = high
                low_part[rows, span] = low
            add_terms(total, span, vector[:, rows], high, low)
        if keep:
            for copy in copies(step):
                copy.start()
        return unused

    lax.fori_loop(0, kept, functools.partial(advance, keep=True), 0)
    lax.fori_loop(kept, steps, functools.partial(advance, keep=False), 0)
    write_terms(total, out_ref)
    for step in range(kept):
        for copy in copies(step):
            copy.wait()


def second_kernel(
    left_ref, right_ref, image_ref, high_ref, low_ref, out_ref, left, right, vector, total, high_part, low_part, come
):
    steps, kept = vector.shape[1] // STEP, high_part.shape[0] // STEP

    def copies(step):
        rows = rows_of(step)
        return [
            pltpu.make_async_copy(ref.at[rows], part.at[rows], come.at[place, step])
            for place, (part, ref) in enumerate([(high_part, high_ref), (low_part, low_ref)])
        ]

    for step in range(kept):
        for copy in copies(step):
            copy.start()
    write_right(right_ref, right)
    write_left(left_ref, left, kept * STEP // LANES)
    split_vector(lambda block: image_ref[block], vector)
    total[...] = jnp.zeros_like(total)

    def compute(step, unused):
        for span in spans(total):
            high, low = parts_of(left[rows_of(step - kept), :], right[:, span])
            add_terms(total, span, vector[:, rows_of(step)], high, low)
        return unused

    def multiply(step, unused):
        rows = rows_of(step)
        for copy in copies(step):
            copy.wait()
        for span in spans(total):
            add_terms(total, span, vector[:, rows], high_part[rows, span], low_part[rows, span])
        return unused

    lax.fori_loop(kept, steps, compute, 0)
    lax.fori_loop(0, kept, multiply, 0)
    write_terms(total, out_ref)
    square = jnp.zeros((NRHS, LANES), jnp.float32)
    product = jnp.zeros((NRHS, LANES), jnp.float32)
    for block in range(left_ref.shape[0]):
        target = left_ref[block, NFEAT:, :]
        square += target * target
        product += target * image_ref[block]
    empty = jnp.zeros((LANES - 2 * NRHS, LANES), jnp.float32)
    turned = jnp.concatenate([square, product, empty], axis=0).T
    row = jnp.sum(turned, axis=0, keepdims=True)
    for block in range(out_ref.shape[0]):
        out_ref[block, NRHS:, :] = jnp.broadcast_to(row, (SUMS, LANES))


def known_kernel(scale_ref, points_ref, targets_ref, scaled_ref, spread_ref):
    for feature in range(NFEAT):
        row = slice(feature, feature + 1)
        scaled_ref[row, :] = points_ref[row, :] * scale_ref[feature]
    for block in range(spread_ref.shape[0]):
        spread_ref[block, :NFEAT, :] = scaled_ref[...]
        spread_ref[block, NFEAT:, :] = targets_ref[...]


def image_kernel(noise_ref, targets_ref, terms_ref, image_ref, spread_ref):
    for place in range(NRHS):
        row = slice(place, place + 1)
        image_ref[row, :] = targets_ref[row, :] * noise_ref[place]
    image = image_ref[...]
    for block in range(terms_ref.shape[0]):
        image += terms_ref[block]
    image_ref[...] = image
    for block in range(spread_ref.shape[0]):
        spread_ref[block] = image


VMEM_BLOCK = pl.BlockSpec(memory_space=pltpu.VMEM)


ANY_BLOCK = pl.BlockSpec(memory_space=pl.ANY)
SMEM_BLOCK = pl.BlockSpec(memory_space=pltpu.SMEM)


def spread_known(inverse_scale, points, targets, count):
    return pl.pallas_call(
        known_kernel,
        out_shape=[
            jax.ShapeDtypeStruct(points.shape, jnp.float32),
            jax.ShapeDtypeStruct((count, NFEAT + NRHS, LANES), jnp.float32),
        ],
        in_specs=[SMEM_BLOCK, VMEM_BLOCK, VMEM_BLOCK],
        out_specs=[VMEM_BLOCK] * 2,
        compiler_params=pltpu.CompilerParams(vmem_limit_bytes=SMALL_LIMIT),
    )(inverse_scale, points, targets)


def spread_image(noise_var, targets, terms, count):
    return pl.pallas_call(
        image_kernel,
        out_shape=[
            jax.ShapeDtypeStruct(targets.shape, jnp.float32),
            jax.ShapeDtypeStruct((count,) + targets.shape, jnp.float32),
        ],
        in_specs=[SMEM_BLOCK, VMEM_BLOCK, VMEM_BLOCK],
        out_specs=[VMEM_BLOCK] * 2,
        compiler_params=pltpu.CompilerParams(vmem_limit_bytes=SMALL_LIMIT),
    )(noise_var, targets, terms)


def scratch(left_count, feature_count, right_count):
    part = pltpu.VMEM((KEPT * STEP, right_count), jnp.bfloat16)
    return [
        pltpu.VMEM((feature_count, FEATURE_ROWS), jnp.bfloat16),
        pltpu.VMEM((FEATURE_ROWS, right_count), jnp.bfloat16),
        pltpu.VMEM((2 * NRHS, left_count), jnp.bfloat16),
        pltpu.VMEM((3 * NRHS, right_count), jnp.float32),
        part,
        part,
        pltpu.SemaphoreType.DMA((2, KEPT)),
    ]


def first_product(left, right):
    left_count, right_count = left.shape[0] * LANES, right.shape[0] * LANES
    part = jax.ShapeDtypeStruct((KEPT * STEP, right_count), jnp.bfloat16)
    return pl.pallas_call(
        first_kernel,
        out_shape=[jax.ShapeDtypeStruct((right.shape[0], NRHS, LANES), jnp.float32), part, part],
        in_specs=[VMEM_BLOCK] * 2,
        out_specs=[VMEM_BLOCK, ANY_BLOCK, ANY_BLOCK],
        scratch_shapes=scratch(left_count, left_count, right_count),
        compiler_params=pltpu.CompilerParams(vmem_limit_bytes=VMEM_LIMIT),
    )(left, right)


def second_product(left, right, image, high, low):
    left_count, right_count = left.shape[0] * LANES, right.shape[0] * LANES
    return pl.pallas_call(
        second_kernel,
        out_shape=jax.ShapeDtypeStruct((right.shape[0], NRHS + SUMS, LANES), jnp.float32),
        in_specs=[VMEM_BLOCK] * 3 + [ANY_BLOCK] * 2,
        out_specs=VMEM_BLOCK,
        scratch_shapes=scratch(left_count, left_count - KEPT * STEP, right_count),
        compiler_params=pltpu.CompilerParams(vmem_limit_bytes=VMEM_LIMIT),
    )(left, right, image, high, low)


def exchange(blocks, axis):
    return lax.all_to_all(blocks, axis, 0, 0, tiled=True)


def gather(block, axis, count):
    return exchange(jnp.broadcast_to(block[None], (count,) + block.shape), axis)


def tile_of(sums):
    stacked = jnp.stack(sums)
    return jnp.pad(stacked, ((0, SUMS - stacked.shape[0]), (0, LANES - NRHS)))


def inner(left, right):
    return jnp.sum(left * right, axis=1)


def on_device(rows, cols, points, inverse_scale, targets, noise_var):
    scaled, spread = spread_known(inverse_scale, points, targets, rows)
    left = exchange(spread, "row")
    right = lax.all_gather(scaled, "col", axis=0)

    partial, high, low = first_product(left, right)
    image, spread = spread_image(noise_var, targets, exchange(partial, "col"), rows)
    partial = second_product(left, right, exchange(spread, "row"), high, low)
    noise = noise_var[:, None]
    reduced = jnp.sum(exchange(partial, "col"), axis=0)
    image_image = reduced[:NRHS] + noise * image

    norm_now, curvature = reduced[NRHS, :NRHS], reduced[NRHS, NRHS : 2 * NRHS]
    step_size = (norm_now / curvature)[:, None]
    residual = targets - step_size * image
    residual_image = image - step_size * image_image
    sums = tile_of([inner(residual, residual), inner(residual, residual_image), inner(residual, image)])
    sums = jnp.sum(gather(sums, "col", cols), axis=0)
    sums = jnp.sum(gather(sums, "row", rows), axis=0)
    norm_next = sums[0, :NRHS]
    ratio = norm_next / norm_now
    next_curvature = sums[1, :NRHS] + ratio * (2.0 * sums[2, :NRHS] + ratio * curvature)
    next_step = (norm_next / next_curvature)[:, None]
    ratio = ratio[:, None]
    solution = step_size * targets + next_step * (residual + ratio * targets)
    residual = residual - next_step * (residual_image + ratio * image)
    return (solution, residual)


def solution(mesh):
    return jax.shard_map(
        functools.partial(on_device, mesh.shape["row"], mesh.shape["col"]),
        mesh=mesh,
        in_specs=(P(None, ("row", "col")), P(), P(None, ("row", "col")), P()),
        out_specs=(P(None, ("row", "col")), P(None, ("row", "col"))),
        check_vma=False,
    )
```

```python
import functools
import math

import jax
import jax.numpy as jnp
from jax import lax
from jax.experimental import pallas as pl
from jax.experimental.pallas import tpu as pltpu
from jax.sharding import PartitionSpec as P

LANES = 128
NFEAT = 8
NRHS = 16
SUMS = 8
FEATURE_ROWS = 64
ROOT_LOG2E = math.sqrt(math.log2(math.e))
WIDE = 256
VMEM_LIMIT = 40 << 20


def pieces(value):
    high = value.astype(jnp.bfloat16).astype(jnp.float32)
    rest = value - high
    middle = rest.astype(jnp.bfloat16).astype(jnp.float32)
    low = (rest - middle).astype(jnp.bfloat16).astype(jnp.float32)
    return high, middle, low


def features(scaled, is_left):
    z = scaled * ROOT_LOG2E
    high, middle, low = pieces(z)
    norm_pieces = pieces(-0.5 * jnp.sum(z * z, axis=0, keepdims=True))
    row = lax.broadcasted_iota(jnp.int32, z.shape, 0)
    start = 0 if is_left else 3
    norms = jnp.where((row < 6) & ((row < start) | (row >= start + 3)), 1.0, 0.0)
    for place, piece in enumerate(norm_pieces):
        norms = jnp.where(row == start + place, piece, norms)
    if is_left:
        parts = [high, high, middle, middle, high, low]
    else:
        parts = [high, middle, high, middle, low, high]
    return jnp.concatenate(parts + [norms, jnp.zeros_like(z)], axis=0)


def dot(left, right):
    return lax.dot_general(left, right, (((1,), (0,)), ((), ())), preferred_element_type=jnp.float32)


def split_vector(value_of, vector):
    for block in range(vector.shape[1] // LANES):
        span = pl.ds(block * LANES, LANES)
        vector[:, span] = jnp.concatenate(pieces(value_of(block))[:2], axis=0).astype(jnp.bfloat16)


def write_right(right_ref, right):
    for block in range(right_ref.shape[0]):
        span = pl.ds(block * LANES, LANES)
        right[:, span] = features(right_ref[block], False).astype(jnp.bfloat16)


def write_left(left_ref, left):
    for block in range(left_ref.shape[0]):
        span = pl.ds(block * LANES, LANES)
        left[span, :] = features(left_ref[block, :NFEAT, :], True).T.astype(jnp.bfloat16)


def write_terms(total, out_ref):
    for block in range(out_ref.shape[0]):
        terms = total[:, pl.ds(block * LANES, LANES)]
        out_ref[block, :NRHS, :] = terms[:NRHS] + terms[NRHS : 2 * NRHS] + terms[2 * NRHS :]


def parts_of(left_block, right_block):
    kernel = jnp.exp2(dot(left_block, right_block))
    high = kernel.astype(jnp.bfloat16)
    return high, (kernel - high.astype(jnp.float32)).astype(jnp.bfloat16)


def write_total(vector, high, low, span, total):
    total[: 2 * NRHS, span] = dot(vector[...], high)
    total[2 * NRHS :, span] = dot(vector[:NRHS, :], low)


def multiply(left_ref, right_ref, value_of, out_ref, left, right, vector, total):
    write_right(right_ref, right)
    write_left(left_ref, left)
    split_vector(value_of, vector)
    for place in range(total.shape[1] // WIDE):
        span = pl.ds(place * WIDE, WIDE)
        high, low = parts_of(left[...], right[:, span])
        write_total(vector, high, low, span, total)
    write_terms(total, out_ref)


def first_kernel(left_ref, right_ref, out_ref, *scratch_refs):
    multiply(left_ref, right_ref, lambda block: left_ref[block, NFEAT:, :], out_ref, *scratch_refs)


def second_kernel(left_ref, right_ref, image_ref, out_ref, *scratch_refs):
    multiply(left_ref, right_ref, lambda block: image_ref[block], out_ref, *scratch_refs)
    square = jnp.zeros((NRHS, LANES), jnp.float32)
    product = jnp.zeros((NRHS, LANES), jnp.float32)
    for block in range(left_ref.shape[0]):
        target = left_ref[block, NFEAT:, :]
        square += target * target
        product += target * image_ref[block]
    empty = jnp.zeros((LANES - 2 * NRHS, LANES), jnp.float32)
    turned = jnp.concatenate([square, product, empty], axis=0).T
    row = jnp.sum(turned, axis=0, keepdims=True)
    for block in range(out_ref.shape[0]):
        out_ref[block, NRHS:, :] = jnp.broadcast_to(row, (SUMS, LANES))


VMEM_BLOCK = pl.BlockSpec(memory_space=pltpu.VMEM)


def image_terms(body, rows, left, right, *others):
    left_count, right_count = left.shape[0] * LANES, right.shape[0] * LANES
    return pl.pallas_call(
        body,
        out_shape=jax.ShapeDtypeStruct((right.shape[0], rows, LANES), jnp.float32),
        in_specs=[VMEM_BLOCK] * (2 + len(others)),
        out_specs=VMEM_BLOCK,
        scratch_shapes=[
            pltpu.VMEM((left_count, FEATURE_ROWS), jnp.bfloat16),
            pltpu.VMEM((FEATURE_ROWS, right_count), jnp.bfloat16),
            pltpu.VMEM((2 * NRHS, left_count), jnp.bfloat16),
            pltpu.VMEM((3 * NRHS, right_count), jnp.float32),
        ],
        compiler_params=pltpu.CompilerParams(vmem_limit_bytes=VMEM_LIMIT),
    )(left, right, *others)


def exchange(blocks, axis):
    return lax.all_to_all(blocks, axis, 0, 0, tiled=True)


def gather(block, axis, count):
    return exchange(jnp.broadcast_to(block[None], (count,) + block.shape), axis)


def tile_of(sums):
    stacked = jnp.stack(sums)
    return jnp.pad(stacked, ((0, SUMS - stacked.shape[0]), (0, LANES - NRHS)))


def inner(left, right):
    return jnp.sum(left * right, axis=1)


def on_device(rows, cols, points, inverse_scale, targets, noise_var):
    noise = noise_var[:, None]
    known = lax.optimization_barrier(jnp.concatenate([points * inverse_scale[:, None], targets], axis=0))
    targets = known[NFEAT:]
    left = gather(known, "row", rows)
    right = lax.all_gather(known[:NFEAT], "col", axis=0)

    partial = image_terms(first_kernel, NRHS, left, right)
    image = jnp.sum(exchange(partial, "col"), axis=0) + noise * targets
    partial = image_terms(second_kernel, NRHS + SUMS, left, right, gather(image, "row", rows))
    reduced = jnp.sum(exchange(partial, "col"), axis=0)
    image_image = reduced[:NRHS] + noise * image

    norm_now, curvature = reduced[NRHS, :NRHS], reduced[NRHS, NRHS : 2 * NRHS]
    step_size = (norm_now / curvature)[:, None]
    residual = targets - step_size * image
    residual_image = image - step_size * image_image
    sums = tile_of([inner(residual, residual), inner(residual, residual_image), inner(residual, image)])
    sums = jnp.sum(gather(sums, "col", cols), axis=0)
    sums = jnp.sum(gather(sums, "row", rows), axis=0)
    norm_next = sums[0, :NRHS]
    ratio = norm_next / norm_now
    next_curvature = sums[1, :NRHS] + ratio * (2.0 * sums[2, :NRHS] + ratio * curvature)
    next_step = (norm_next / next_curvature)[:, None]
    ratio = ratio[:, None]
    solution = step_size * targets + next_step * (residual + ratio * targets)
    residual = residual - next_step * (residual_image + ratio * image)
    return (solution, residual)


def solution(mesh):
    return jax.shard_map(
        functools.partial(on_device, mesh.shape["row"], mesh.shape["col"]),
        mesh=mesh,
        in_specs=(P(None, ("row", "col")), P(), P(None, ("row", "col")), P()),
        out_specs=(P(None, ("row", "col")), P(None, ("row", "col"))),
        check_vma=False,
    )
```

```python
import functools
import math

import jax
import jax.numpy as jnp
from jax import lax
from jax.experimental import pallas as pl
from jax.experimental.pallas import tpu as pltpu
from jax.sharding import PartitionSpec as P

LANES = 128
NFEAT = 8
NRHS = 16
SUMS = 8
FEATURE_ROWS = 64
ROOT_LOG2E = math.sqrt(math.log2(math.e))
WIDE = 256
CHUNK = 512
VMEM_LIMIT = 40 << 20


def pieces(value):
    high = value.astype(jnp.bfloat16).astype(jnp.float32)
    rest = value - high
    middle = rest.astype(jnp.bfloat16).astype(jnp.float32)
    low = (rest - middle).astype(jnp.bfloat16).astype(jnp.float32)
    return high, middle, low


def features(scaled, is_left):
    z = scaled * ROOT_LOG2E
    high, middle, low = pieces(z)
    norm_pieces = pieces(-0.5 * jnp.sum(z * z, axis=0, keepdims=True))
    row = lax.broadcasted_iota(jnp.int32, z.shape, 0)
    start = 0 if is_left else 3
    norms = jnp.where((row < 6) & ((row < start) | (row >= start + 3)), 1.0, 0.0)
    for place, piece in enumerate(norm_pieces):
        norms = jnp.where(row == start + place, piece, norms)
    if is_left:
        parts = [high, high, middle, middle, high, low]
    else:
        parts = [high, middle, high, middle, low, high]
    return jnp.concatenate(parts + [norms, jnp.zeros_like(z)], axis=0)


def dot(left, right):
    return lax.dot_general(left, right, (((1,), (0,)), ((), ())), preferred_element_type=jnp.float32)


def split_vector(value_of, vector):
    for block in range(vector.shape[1] // LANES):
        span = pl.ds(block * LANES, LANES)
        vector[:, span] = jnp.concatenate(pieces(value_of(block))[:2], axis=0).astype(jnp.bfloat16)


def write_right(right_ref, right):
    for block in range(right_ref.shape[0]):
        span = pl.ds(block * LANES, LANES)
        right[:, span] = features(right_ref[block], False).astype(jnp.bfloat16)


def write_left(left_ref, left):
    for block in range(left_ref.shape[0]):
        span = pl.ds(block * LANES, LANES)
        left[span, :] = features(left_ref[block, :NFEAT, :], True).T.astype(jnp.bfloat16)


def write_terms(total, out_ref):
    for block in range(out_ref.shape[0]):
        terms = total[:, pl.ds(block * LANES, LANES)]
        out_ref[block, :NRHS, :] = terms[:NRHS] + terms[NRHS : 2 * NRHS] + terms[2 * NRHS :]


def parts_of(left_block, right_block):
    kernel = jnp.exp2(dot(left_block, right_block))
    high = kernel.astype(jnp.bfloat16)
    return high, (kernel - high.astype(jnp.float32)).astype(jnp.bfloat16)


def chunk_terms(left, right, vector, rows, span):
    high, low = parts_of(left[rows, :], right[:, span])
    return jnp.concatenate([dot(vector[:, rows], high), dot(vector[:NRHS, rows], low)], axis=0)


def multiply(left_ref, right_ref, value_of, out_ref, left, right, vector, total):
    write_right(right_ref, right)
    write_left(left_ref, left)
    split_vector(value_of, vector)
    for place in range(total.shape[1] // WIDE):
        span = pl.ds(place * WIDE, WIDE)
        terms = [chunk_terms(left, right, vector, pl.ds(begin, CHUNK), span) for begin in range(0, left.shape[0], CHUNK)]
        total[:, span] = functools.reduce(jnp.add, terms)
    write_terms(total, out_ref)


def first_kernel(left_ref, right_ref, out_ref, *scratch_refs):
    multiply(left_ref, right_ref, lambda block: left_ref[block, NFEAT:, :], out_ref, *scratch_refs)


def second_kernel(left_ref, right_ref, image_ref, out_ref, *scratch_refs):
    multiply(left_ref, right_ref, lambda block: image_ref[block], out_ref, *scratch_refs)
    square = jnp.zeros((NRHS, LANES), jnp.float32)
    product = jnp.zeros((NRHS, LANES), jnp.float32)
    for block in range(left_ref.shape[0]):
        target = left_ref[block, NFEAT:, :]
        square += target * target
        product += target * image_ref[block]
    empty = jnp.zeros((LANES - 2 * NRHS, LANES), jnp.float32)
    turned = jnp.concatenate([square, product, empty], axis=0).T
    row = jnp.sum(turned, axis=0, keepdims=True)
    for block in range(out_ref.shape[0]):
        out_ref[block, NRHS:, :] = jnp.broadcast_to(row, (SUMS, LANES))


VMEM_BLOCK = pl.BlockSpec(memory_space=pltpu.VMEM)


def image_terms(body, rows, left, right, *others):
    left_count, right_count = left.shape[0] * LANES, right.shape[0] * LANES
    return pl.pallas_call(
        body,
        out_shape=jax.ShapeDtypeStruct((right.shape[0], rows, LANES), jnp.float32),
        in_specs=[VMEM_BLOCK] * (2 + len(others)),
        out_specs=VMEM_BLOCK,
        scratch_shapes=[
            pltpu.VMEM((left_count, FEATURE_ROWS), jnp.bfloat16),
            pltpu.VMEM((FEATURE_ROWS, right_count), jnp.bfloat16),
            pltpu.VMEM((2 * NRHS, left_count), jnp.bfloat16),
            pltpu.VMEM((3 * NRHS, right_count), jnp.float32),
        ],
        compiler_params=pltpu.CompilerParams(vmem_limit_bytes=VMEM_LIMIT),
    )(left, right, *others)


def exchange(blocks, axis):
    return lax.all_to_all(blocks, axis, 0, 0, tiled=True)


def gather(block, axis, count):
    return exchange(jnp.broadcast_to(block[None], (count,) + block.shape), axis)


def row_of(sums):
    return jnp.pad(jnp.concatenate(sums), (0, LANES - NRHS * len(sums)))[None]


def inner(left, right):
    return jnp.sum(left * right, axis=1)


def on_device(rows, cols, points, inverse_scale, targets, noise_var):
    noise = noise_var[:, None]
    known = jnp.concatenate([points * inverse_scale[:, None], targets], axis=0)
    known, noise_terms = lax.optimization_barrier((known, noise * targets))
    targets = known[NFEAT:]
    left = gather(known, "row", rows)
    right = lax.all_gather(known[:NFEAT], "col", axis=0)

    partial = image_terms(first_kernel, NRHS, left, right)
    image = jnp.sum(exchange(partial, "col"), axis=0) + noise_terms
    partial = image_terms(second_kernel, NRHS + SUMS, left, right, gather(image, "row", rows))
    reduced = jnp.sum(exchange(partial, "col"), axis=0)
    image_image = reduced[:NRHS] + noise * image

    norm_now, curvature = reduced[NRHS, :NRHS], reduced[NRHS, NRHS : 2 * NRHS]
    step_size = (norm_now / curvature)[:, None]
    residual = targets - step_size * image
    residual_image = image - step_size * image_image
    sums = row_of([inner(residual, residual), inner(residual, residual_image), inner(residual, image)])
    sums = jnp.sum(gather(sums, "col", cols), axis=0)
    sums = jnp.sum(gather(sums, "row", rows), axis=0)[0]
    norm_next = sums[:NRHS]
    ratio = norm_next / norm_now
    next_curvature = sums[NRHS : 2 * NRHS] + ratio * (2.0 * sums[2 * NRHS : 3 * NRHS] + ratio * curvature)
    next_step = (norm_next / next_curvature)[:, None]
    ratio = ratio[:, None]
    solution = step_size * targets + next_step * (residual + ratio * targets)
    residual = residual - next_step * (residual_image + ratio * image)
    return (solution, residual)


def solution(mesh):
    return jax.shard_map(
        functools.partial(on_device, mesh.shape["row"], mesh.shape["col"]),
        mesh=mesh,
        in_specs=(P(None, ("row", "col")), P(), P(None, ("row", "col")), P()),
        out_specs=(P(None, ("row", "col")), P(None, ("row", "col"))),
        check_vma=False,
    )
```

```python
import functools
import math

import jax
import jax.numpy as jnp
from jax import lax
from jax.experimental import pallas as pl
from jax.experimental.pallas import tpu as pltpu
from jax.sharding import PartitionSpec as P

AXES = ("y", "x", "z", "core")
SHAPE = (8, 4, 8, 2)
ROW = ("x", "z")
COL = ("y", "core")
LANES = 128
NFEAT = 8
NRHS = 16
SUMS = 8
FEATURE_ROWS = 64
ROOT_LOG2E = math.sqrt(math.log2(math.e))
WIDE = 256
CHUNK = 512
VMEM_LIMIT = 40 << 20


def pieces(value):
    high = value.astype(jnp.bfloat16).astype(jnp.float32)
    rest = value - high
    middle = rest.astype(jnp.bfloat16).astype(jnp.float32)
    low = (rest - middle).astype(jnp.bfloat16).astype(jnp.float32)
    return high, middle, low


def features(scaled, is_left):
    z = scaled * ROOT_LOG2E
    high, middle, low = pieces(z)
    norm_pieces = pieces(-0.5 * jnp.sum(z * z, axis=0, keepdims=True))
    row = lax.broadcasted_iota(jnp.int32, z.shape, 0)
    start = 0 if is_left else 3
    norms = jnp.where((row < 6) & ((row < start) | (row >= start + 3)), 1.0, 0.0)
    for place, piece in enumerate(norm_pieces):
        norms = jnp.where(row == start + place, piece, norms)
    if is_left:
        parts = [high, high, middle, middle, high, low]
    else:
        parts = [high, middle, high, middle, low, high]
    return jnp.concatenate(parts + [norms, jnp.zeros_like(z)], axis=0)


def dot(left, right):
    return lax.dot_general(left, right, (((1,), (0,)), ((), ())), preferred_element_type=jnp.float32)


def split_vector(value_of, vector):
    for block in range(vector.shape[1] // LANES):
        span = pl.ds(block * LANES, LANES)
        vector[:, span] = jnp.concatenate(pieces(value_of(block))[:2], axis=0).astype(jnp.bfloat16)


def write_right(right_ref, right):
    for block in range(right_ref.shape[0]):
        span = pl.ds(block * LANES, LANES)
        right[:, span] = features(right_ref[block], False).astype(jnp.bfloat16)


def write_left(left_ref, left):
    for block in range(left_ref.shape[0]):
        span = pl.ds(block * LANES, LANES)
        left[span, :] = features(left_ref[block, :NFEAT, :], True).T.astype(jnp.bfloat16)


def write_terms(total, out_ref):
    for block in range(out_ref.shape[0]):
        terms = total[:, pl.ds(block * LANES, LANES)]
        out_ref[block, :NRHS, :] = terms[:NRHS] + terms[NRHS : 2 * NRHS] + terms[2 * NRHS :]


def parts_of(left_block, right_block):
    kernel = jnp.exp2(dot(left_block, right_block))
    high = kernel.astype(jnp.bfloat16)
    return high, (kernel - high.astype(jnp.float32)).astype(jnp.bfloat16)


def chunk_terms(left, right, vector, rows, span):
    high, low = parts_of(left[rows, :], right[:, span])
    return jnp.concatenate([dot(vector[:, rows], high), dot(vector[:NRHS, rows], low)], axis=0)


def multiply(left_ref, right_ref, value_of, out_ref, left, right, vector, total):
    write_right(right_ref, right)
    write_left(left_ref, left)
    split_vector(value_of, vector)
    for place in range(total.shape[1] // WIDE):
        span = pl.ds(place * WIDE, WIDE)
        terms = [chunk_terms(left, right, vector, pl.ds(begin, CHUNK), span) for begin in range(0, left.shape[0], CHUNK)]
        total[:, span] = functools.reduce(jnp.add, terms)
    write_terms(total, out_ref)


def first_kernel(left_ref, right_ref, out_ref, *scratch_refs):
    multiply(left_ref, right_ref, lambda block: left_ref[block, NFEAT:, :], out_ref, *scratch_refs)


def second_kernel(left_ref, right_ref, image_ref, out_ref, *scratch_refs):
    multiply(left_ref, right_ref, lambda block: image_ref[block], out_ref, *scratch_refs)
    square = jnp.zeros((NRHS, LANES), jnp.float32)
    product = jnp.zeros((NRHS, LANES), jnp.float32)
    for block in range(left_ref.shape[0]):
        target = left_ref[block, NFEAT:, :]
        square += target * target
        product += target * image_ref[block]
    empty = jnp.zeros((LANES - 2 * NRHS, LANES), jnp.float32)
    turned = jnp.concatenate([square, product, empty], axis=0).T
    row = jnp.sum(turned, axis=0, keepdims=True)
    for block in range(out_ref.shape[0]):
        out_ref[block, NRHS:, :] = jnp.broadcast_to(row, (SUMS, LANES))


VMEM_BLOCK = pl.BlockSpec(memory_space=pltpu.VMEM)


def image_terms(body, rows, left, right, *others):
    left_count, right_count = left.shape[0] * LANES, right.shape[0] * LANES
    return pl.pallas_call(
        body,
        out_shape=jax.ShapeDtypeStruct((right.shape[0], rows, LANES), jnp.float32),
        in_specs=[VMEM_BLOCK] * (2 + len(others)),
        out_specs=VMEM_BLOCK,
        scratch_shapes=[
            pltpu.VMEM((left_count, FEATURE_ROWS), jnp.bfloat16),
            pltpu.VMEM((FEATURE_ROWS, right_count), jnp.bfloat16),
            pltpu.VMEM((2 * NRHS, left_count), jnp.bfloat16),
            pltpu.VMEM((3 * NRHS, right_count), jnp.float32),
        ],
        compiler_params=pltpu.CompilerParams(vmem_limit_bytes=VMEM_LIMIT),
    )(left, right, *others)


def exchange(blocks, axis):
    return lax.all_to_all(blocks, axis, 0, 0, tiled=True)


def gather(block, axis, count):
    return exchange(jnp.broadcast_to(block[None], (count,) + block.shape), axis)


def row_of(sums):
    return jnp.pad(jnp.concatenate(sums), (0, LANES - NRHS * len(sums)))[None]


def inner(left, right):
    return jnp.sum(left * right, axis=1)


def on_device(rows, cols, points, inverse_scale, targets, noise_var):
    noise = noise_var[:, None]
    known = jnp.concatenate([points * inverse_scale[:, None], targets], axis=0)
    known = lax.optimization_barrier(known)
    targets = known[NFEAT:]
    left = gather(known, ROW, rows)
    right = lax.all_gather(known[:NFEAT], COL, axis=0)
    right, noise_terms = lax.optimization_barrier((right, noise * targets))

    partial = image_terms(first_kernel, NRHS, left, right)
    image = jnp.sum(exchange(partial, COL), axis=0) + noise_terms
    partial = image_terms(second_kernel, NRHS + SUMS, left, right, gather(image, ROW, rows))
    reduced = jnp.sum(exchange(partial, COL), axis=0)
    image_image = reduced[:NRHS] + noise * image

    norm_now, curvature = reduced[NRHS, :NRHS], reduced[NRHS, NRHS : 2 * NRHS]
    step_size = (norm_now / curvature)[:, None]
    residual = targets - step_size * image
    residual_image = image - step_size * image_image
    sums = row_of([inner(residual, residual), inner(residual, residual_image), inner(residual, image)])
    sums = jnp.sum(gather(sums, COL, cols), axis=0)
    sums = jnp.sum(gather(sums, ROW, rows), axis=0)[0]
    norm_next = sums[:NRHS]
    ratio = norm_next / norm_now
    next_curvature = sums[NRHS : 2 * NRHS] + ratio * (2.0 * sums[2 * NRHS : 3 * NRHS] + ratio * curvature)
    next_step = (norm_next / next_curvature)[:, None]
    ratio = ratio[:, None]
    solution = step_size * targets + next_step * (residual + ratio * targets)
    residual = residual - next_step * (residual_image + ratio * image)
    return (solution, residual)


def size_of(mesh, axes):
    return math.prod(mesh.shape[axis] for axis in axes)


def solution(mesh):
    mesh = jax.sharding.Mesh(mesh.devices.reshape(SHAPE), AXES)
    return jax.shard_map(
        functools.partial(on_device, size_of(mesh, ROW), size_of(mesh, COL)),
        mesh=mesh,
        in_specs=(P(None, AXES), P(), P(None, AXES), P()),
        out_specs=(P(None, AXES), P(None, AXES)),
        check_vma=False,
    )
```

```python
import functools
import math

import jax
import jax.numpy as jnp
from jax import lax
from jax.experimental import pallas as pl
from jax.experimental.pallas import tpu as pltpu
from jax.sharding import PartitionSpec as P

AXES = ("y", "x", "z", "core")
SHAPE = (8, 4, 8, 2)
ROW = ("x", "z")
COL = ("y", "core")
LANES = 128
NFEAT = 8
NRHS = 16
SUMS = 8
FEATURE_ROWS = 64
ROOT_LOG2E = math.sqrt(math.log2(math.e))
WIDE = 256
CHUNK = 512
VMEM_LIMIT = 40 << 20


def pieces(value):
    high = value.astype(jnp.bfloat16).astype(jnp.float32)
    rest = value - high
    middle = rest.astype(jnp.bfloat16).astype(jnp.float32)
    low = (rest - middle).astype(jnp.bfloat16).astype(jnp.float32)
    return high, middle, low


def features(scaled, is_left):
    z = scaled * ROOT_LOG2E
    high, middle, low = pieces(z)
    norm_pieces = pieces(-0.5 * jnp.sum(z * z, axis=0, keepdims=True))
    row = lax.broadcasted_iota(jnp.int32, z.shape, 0)
    start = 0 if is_left else 3
    norms = jnp.where((row < 6) & ((row < start) | (row >= start + 3)), 1.0, 0.0)
    for place, piece in enumerate(norm_pieces):
        norms = jnp.where(row == start + place, piece, norms)
    if is_left:
        parts = [high, high, middle, middle, high, low]
    else:
        parts = [high, middle, high, middle, low, high]
    return jnp.concatenate(parts + [norms, jnp.zeros_like(z)], axis=0)


def dot(left, right):
    return lax.dot_general(left, right, (((1,), (0,)), ((), ())), preferred_element_type=jnp.float32)


def split_vector(value_of, vector):
    for block in range(vector.shape[1] // LANES):
        span = pl.ds(block * LANES, LANES)
        vector[:, span] = jnp.concatenate(pieces(value_of(block))[:2], axis=0).astype(jnp.bfloat16)


def write_right(right_ref, right):
    for block in range(right_ref.shape[0]):
        span = pl.ds(block * LANES, LANES)
        right[:, span] = features(right_ref[block], False).astype(jnp.bfloat16)


def write_left(left_ref, left):
    for block in range(left_ref.shape[0]):
        span = pl.ds(block * LANES, LANES)
        left[span, :] = features(left_ref[block, :NFEAT, :], True).T.astype(jnp.bfloat16)


def write_terms(total, out_ref):
    for block in range(out_ref.shape[0]):
        terms = total[:, pl.ds(block * LANES, LANES)]
        out_ref[block, :NRHS, :] = terms[:NRHS] + terms[NRHS : 2 * NRHS] + terms[2 * NRHS :]


def parts_of(left_block, right_block):
    kernel = jnp.exp2(dot(left_block, right_block))
    high = kernel.astype(jnp.bfloat16)
    return high, (kernel - high.astype(jnp.float32)).astype(jnp.bfloat16)


def chunk_terms(left, right, vector, rows, span):
    high, low = parts_of(left[rows, :], right[:, span])
    return jnp.concatenate([dot(vector[:, rows], high), dot(vector[:NRHS, rows], low)], axis=0)


def multiply(value_of, out_ref, left, right, vector, total):
    split_vector(value_of, vector)
    for place in range(total.shape[1] // WIDE):
        span = pl.ds(place * WIDE, WIDE)
        terms = [chunk_terms(left, right, vector, pl.ds(begin, CHUNK), span) for begin in range(0, left.shape[0], CHUNK)]
        total[:, span] = functools.reduce(jnp.add, terms)
    write_terms(total, out_ref)


def first_kernel(left_ref, right_ref, out_ref, left, right, vector, total):
    write_right(right_ref, right)
    write_left(left_ref, left)
    multiply(lambda block: left_ref[block, NFEAT:, :], out_ref, left, right, vector, total)


def second_kernel(left_ref, image_ref, left, right, out_ref, vector, total):
    multiply(lambda block: image_ref[block], out_ref, left, right, vector, total)
    square = jnp.zeros((NRHS, LANES), jnp.float32)
    product = jnp.zeros((NRHS, LANES), jnp.float32)
    for block in range(left_ref.shape[0]):
        target = left_ref[block, NFEAT:, :]
        square += target * target
        product += target * image_ref[block]
    empty = jnp.zeros((LANES - 2 * NRHS, LANES), jnp.float32)
    turned = jnp.concatenate([square, product, empty], axis=0).T
    row = jnp.sum(turned, axis=0, keepdims=True)
    for block in range(out_ref.shape[0]):
        out_ref[block, NRHS:, :] = jnp.broadcast_to(row, (SUMS, LANES))


VMEM_BLOCK = pl.BlockSpec(memory_space=pltpu.VMEM)


def product_scratch(left_count, right_count):
    return [
        pltpu.VMEM((2 * NRHS, left_count), jnp.bfloat16),
        pltpu.VMEM((3 * NRHS, right_count), jnp.float32),
    ]


def first_terms(left, right):
    left_count, right_count = left.shape[0] * LANES, right.shape[0] * LANES
    return pl.pallas_call(
        first_kernel,
        out_shape=[
            jax.ShapeDtypeStruct((right.shape[0], NRHS, LANES), jnp.float32),
            jax.ShapeDtypeStruct((left_count, FEATURE_ROWS), jnp.bfloat16),
            jax.ShapeDtypeStruct((FEATURE_ROWS, right_count), jnp.bfloat16),
        ],
        in_specs=[VMEM_BLOCK] * 2,
        out_specs=[VMEM_BLOCK] * 3,
        scratch_shapes=product_scratch(left_count, right_count),
        compiler_params=pltpu.CompilerParams(vmem_limit_bytes=VMEM_LIMIT),
    )(left, right)


def second_terms(left, image, left_features, right_features):
    left_count, right_count = left_features.shape[0], right_features.shape[1]
    return pl.pallas_call(
        second_kernel,
        out_shape=jax.ShapeDtypeStruct((right_count // LANES, NRHS + SUMS, LANES), jnp.float32),
        in_specs=[VMEM_BLOCK] * 4,
        out_specs=VMEM_BLOCK,
        scratch_shapes=product_scratch(left_count, right_count),
        compiler_params=pltpu.CompilerParams(vmem_limit_bytes=VMEM_LIMIT),
    )(left, image, left_features, right_features)


def exchange(blocks, axis):
    return lax.all_to_all(blocks, axis, 0, 0, tiled=True)


def gather(block, axis, count):
    return exchange(jnp.broadcast_to(block[None], (count,) + block.shape), axis)


def row_of(sums):
    return jnp.pad(jnp.concatenate(sums), (0, LANES - NRHS * len(sums)))[None]


def inner(left, right):
    return jnp.sum(left * right, axis=1)


def on_device(rows, cols, points, inverse_scale, targets, noise_var):
    noise = noise_var[:, None]
    known = jnp.concatenate([points * inverse_scale[:, None], targets], axis=0)
    known = lax.optimization_barrier(known)
    targets = known[NFEAT:]
    left = gather(known, ROW, rows)
    right = lax.all_gather(known[:NFEAT], COL, axis=0)
    right, noise_terms = lax.optimization_barrier((right, noise * targets))

    partial, *kept = first_terms(left, right)
    image = jnp.sum(exchange(partial, COL), axis=0) + noise_terms
    partial = second_terms(left, gather(image, ROW, rows), *kept)
    reduced = jnp.sum(exchange(partial, COL), axis=0)
    image_image = reduced[:NRHS] + noise * image

    norm_now, curvature = reduced[NRHS, :NRHS], reduced[NRHS, NRHS : 2 * NRHS]
    step_size = (norm_now / curvature)[:, None]
    residual = targets - step_size * image
    residual_image = image - step_size * image_image
    sums = row_of([inner(residual, residual), inner(residual, residual_image), inner(residual, image)])
    sums = jnp.sum(gather(sums, COL, cols), axis=0)
    sums = jnp.sum(gather(sums, ROW, rows), axis=0)[0]
    norm_next = sums[:NRHS]
    ratio = norm_next / norm_now
    next_curvature = sums[NRHS : 2 * NRHS] + ratio * (2.0 * sums[2 * NRHS : 3 * NRHS] + ratio * curvature)
    next_step = (norm_next / next_curvature)[:, None]
    ratio = ratio[:, None]
    solution = step_size * targets + next_step * (residual + ratio * targets)
    residual = residual - next_step * (residual_image + ratio * image)
    return (solution, residual)


def size_of(mesh, axes):
    return math.prod(mesh.shape[axis] for axis in axes)


def solution(mesh):
    mesh = jax.sharding.Mesh(mesh.devices.reshape(SHAPE), AXES)
    return jax.shard_map(
        functools.partial(on_device, size_of(mesh, ROW), size_of(mesh, COL)),
        mesh=mesh,
        in_specs=(P(None, AXES), P(), P(None, AXES), P()),
        out_specs=(P(None, AXES), P(None, AXES)),
        check_vma=False,
    )
```

```python
import functools
import math

import jax
import jax.numpy as jnp
from jax import lax
from jax.experimental import pallas as pl
from jax.experimental.pallas import tpu as pltpu
from jax.sharding import PartitionSpec as P

AXES = ("y", "x", "z", "core")
SHAPE = (8, 4, 8, 2)
ROW = ("x", "z")
COL = ("y", "core")
LANES = 128
NFEAT = 8
NRHS = 16
SUMS = 8
FEATURE_ROWS = 64
ROOT_LOG2E = math.sqrt(math.log2(math.e))
WIDE = 256
CHUNK = 512
VMEM_LIMIT = 40 << 20


def pieces(value):
    high = value.astype(jnp.bfloat16).astype(jnp.float32)
    rest = value - high
    middle = rest.astype(jnp.bfloat16).astype(jnp.float32)
    low = (rest - middle).astype(jnp.bfloat16).astype(jnp.float32)
    return high, middle, low


def features(scaled, is_left):
    z = scaled * ROOT_LOG2E
    high, middle, low = pieces(z)
    norm_pieces = pieces(-0.5 * jnp.sum(z * z, axis=0, keepdims=True))
    row = lax.broadcasted_iota(jnp.int32, z.shape, 0)
    start = 0 if is_left else 3
    norms = jnp.where((row < 6) & ((row < start) | (row >= start + 3)), 1.0, 0.0)
    for place, piece in enumerate(norm_pieces):
        norms = jnp.where(row == start + place, piece, norms)
    if is_left:
        parts = [high, high, middle, middle, high, low]
    else:
        parts = [high, middle, high, middle, low, high]
    return jnp.concatenate(parts + [norms, jnp.zeros_like(z)], axis=0)


def dot(left, right):
    return lax.dot_general(left, right, (((1,), (0,)), ((), ())), preferred_element_type=jnp.float32)


def split_vector(value_of, vector):
    for block in range(vector.shape[1] // LANES):
        span = pl.ds(block * LANES, LANES)
        vector[:, span] = jnp.concatenate(pieces(value_of(block))[:2], axis=0).astype(jnp.bfloat16)


def write_right(right_ref, right):
    for block in range(right_ref.shape[0]):
        span = pl.ds(block * LANES, LANES)
        right[:, span] = features(right_ref[block], False).astype(jnp.bfloat16)


def write_left(left_ref, left):
    for block in range(left_ref.shape[0]):
        span = pl.ds(block * LANES, LANES)
        left[span, :] = features(left_ref[block, :NFEAT, :], True).T.astype(jnp.bfloat16)


def write_terms(total, out_ref):
    for block in range(out_ref.shape[0]):
        terms = total[:, pl.ds(block * LANES, LANES)]
        out_ref[block, :NRHS, :] = terms[:NRHS] + terms[NRHS : 2 * NRHS] + terms[2 * NRHS :]


def parts_of(left_block, right_block):
    kernel = jnp.exp2(dot(left_block, right_block))
    high = kernel.astype(jnp.bfloat16)
    return high, (kernel - high.astype(jnp.float32)).astype(jnp.bfloat16)


def chunk_terms(left, right, vector, rows, span):
    high, low = parts_of(left[rows, :], right[:, span])
    return jnp.concatenate([dot(vector[:, rows], high), dot(vector[:NRHS, rows], low)], axis=0)


def multiply(left_ref, right_ref, value_of, out_ref, left, right, vector, total):
    write_right(right_ref, right)
    write_left(left_ref, left)
    split_vector(value_of, vector)
    for place in range(total.shape[1] // WIDE):
        span = pl.ds(place * WIDE, WIDE)
        terms = [chunk_terms(left, right, vector, pl.ds(begin, CHUNK), span) for begin in range(0, left.shape[0], CHUNK)]
        total[:, span] = functools.reduce(jnp.add, terms)
    write_terms(total, out_ref)


def first_kernel(left_ref, right_ref, out_ref, *scratch_refs):
    multiply(left_ref, right_ref, lambda block: left_ref[block, NFEAT:, :], out_ref, *scratch_refs)


def second_kernel(left_ref, right_ref, image_ref, out_ref, *scratch_refs):
    multiply(left_ref, right_ref, lambda block: image_ref[block], out_ref, *scratch_refs)
    square = jnp.zeros((NRHS, LANES), jnp.float32)
    product = jnp.zeros((NRHS, LANES), jnp.float32)
    for block in range(left_ref.shape[0]):
        target = left_ref[block, NFEAT:, :]
        square += target * target
        product += target * image_ref[block]
    empty = jnp.zeros((LANES - 2 * NRHS, LANES), jnp.float32)
    turned = jnp.concatenate([square, product, empty], axis=0).T
    row = jnp.sum(turned, axis=0, keepdims=True)
    for block in range(out_ref.shape[0]):
        out_ref[block, NRHS:, :] = jnp.broadcast_to(row, (SUMS, LANES))


VMEM_BLOCK = pl.BlockSpec(memory_space=pltpu.VMEM)


def image_terms(body, rows, left, right, *others):
    left_count, right_count = left.shape[0] * LANES, right.shape[0] * LANES
    return pl.pallas_call(
        body,
        out_shape=jax.ShapeDtypeStruct((right.shape[0], rows, LANES), jnp.float32),
        in_specs=[VMEM_BLOCK] * (2 + len(others)),
        out_specs=VMEM_BLOCK,
        scratch_shapes=[
            pltpu.VMEM((left_count, FEATURE_ROWS), jnp.bfloat16),
            pltpu.VMEM((FEATURE_ROWS, right_count), jnp.bfloat16),
            pltpu.VMEM((2 * NRHS, left_count), jnp.bfloat16),
            pltpu.VMEM((3 * NRHS, right_count), jnp.float32),
        ],
        compiler_params=pltpu.CompilerParams(vmem_limit_bytes=VMEM_LIMIT),
    )(left, right, *others)


def exchange(blocks, axis):
    return lax.all_to_all(blocks, axis, 0, 0, tiled=True)


def gather(block, axis, count):
    return exchange(jnp.broadcast_to(block[None], (count,) + block.shape), axis)


def row_of(sums):
    return jnp.pad(jnp.concatenate(sums), (0, LANES - NRHS * len(sums)))[None]


def inner(left, right):
    return jnp.sum(left * right, axis=1)


def on_device(rows, cols, points, inverse_scale, targets, noise_var):
    noise = noise_var[:, None]
    scaled = points * inverse_scale[:, None]
    spread = [jnp.broadcast_to(block[None], (rows,) + block.shape) for block in (scaled, targets)]
    left = exchange(jnp.concatenate(spread, axis=1), ROW)
    right = lax.all_gather(scaled, COL, axis=0)
    right, noise_terms = lax.optimization_barrier((right, noise * targets))

    partial = image_terms(first_kernel, NRHS, left, right)
    image = jnp.sum(exchange(partial, COL), axis=0) + noise_terms
    partial = image_terms(second_kernel, NRHS + SUMS, left, right, gather(image, ROW, rows))
    reduced = jnp.sum(exchange(partial, COL), axis=0)
    image_image = reduced[:NRHS] + noise * image

    norm_now, curvature = reduced[NRHS, :NRHS], reduced[NRHS, NRHS : 2 * NRHS]
    step_size = (norm_now / curvature)[:, None]
    residual = targets - step_size * image
    residual_image = image - step_size * image_image
    sums = row_of([inner(residual, residual), inner(residual, residual_image), inner(residual, image)])
    sums = jnp.sum(gather(sums, COL, cols), axis=0)
    sums = jnp.sum(gather(sums, ROW, rows), axis=0)[0]
    norm_next = sums[:NRHS]
    ratio = norm_next / norm_now
    next_curvature = sums[NRHS : 2 * NRHS] + ratio * (2.0 * sums[2 * NRHS : 3 * NRHS] + ratio * curvature)
    next_step = (norm_next / next_curvature)[:, None]
    ratio = ratio[:, None]
    solution = step_size * targets + next_step * (residual + ratio * targets)
    residual = residual - next_step * (residual_image + ratio * image)
    return (solution, residual)


def size_of(mesh, axes):
    return math.prod(mesh.shape[axis] for axis in axes)


def solution(mesh):
    mesh = jax.sharding.Mesh(mesh.devices.reshape(SHAPE), AXES)
    return jax.shard_map(
        functools.partial(on_device, size_of(mesh, ROW), size_of(mesh, COL)),
        mesh=mesh,
        in_specs=(P(None, AXES), P(), P(None, AXES), P()),
        out_specs=(P(None, AXES), P(None, AXES)),
        check_vma=False,
    )
```

```python
import functools
import math

import jax
import jax.numpy as jnp
from jax import lax
from jax.experimental import pallas as pl
from jax.experimental.pallas import tpu as pltpu
from jax.sharding import PartitionSpec as P

AXES = ("y", "x", "z", "core")
SHAPE = (8, 4, 8, 2)
ROW = ("z", "x")
COL = ("y", "core")
LANES = 128
NFEAT = 8
NRHS = 16
SUMS = 8
FEATURE_ROWS = 64
ROOT_LOG2E = math.sqrt(math.log2(math.e))
WIDE = 256
CHUNK = 512
VMEM_LIMIT = 40 << 20


def pieces(value):
    high = value.astype(jnp.bfloat16).astype(jnp.float32)
    rest = value - high
    middle = rest.astype(jnp.bfloat16).astype(jnp.float32)
    low = (rest - middle).astype(jnp.bfloat16).astype(jnp.float32)
    return high, middle, low


def features(scaled, is_left):
    z = scaled * ROOT_LOG2E
    high, middle, low = pieces(z)
    norm_pieces = pieces(-0.5 * jnp.sum(z * z, axis=0, keepdims=True))
    row = lax.broadcasted_iota(jnp.int32, z.shape, 0)
    start = 0 if is_left else 3
    norms = jnp.where((row < 6) & ((row < start) | (row >= start + 3)), 1.0, 0.0)
    for place, piece in enumerate(norm_pieces):
        norms = jnp.where(row == start + place, piece, norms)
    if is_left:
        parts = [high, high, middle, middle, high, low]
    else:
        parts = [high, middle, high, middle, low, high]
    return jnp.concatenate(parts + [norms, jnp.zeros_like(z)], axis=0)


def dot(left, right):
    return lax.dot_general(left, right, (((1,), (0,)), ((), ())), preferred_element_type=jnp.float32)


def split_vector(value_of, vector):
    for block in range(vector.shape[1] // LANES):
        span = pl.ds(block * LANES, LANES)
        vector[:, span] = jnp.concatenate(pieces(value_of(block))[:2], axis=0).astype(jnp.bfloat16)


def write_right(right_ref, right):
    for block in range(right_ref.shape[0]):
        span = pl.ds(block * LANES, LANES)
        right[:, span] = features(right_ref[block], False).astype(jnp.bfloat16)


def write_left(left_ref, left):
    for block in range(left_ref.shape[0]):
        span = pl.ds(block * LANES, LANES)
        left[span, :] = features(left_ref[block, :NFEAT, :], True).T.astype(jnp.bfloat16)


def write_terms(total, out_ref):
    for block in range(out_ref.shape[0]):
        terms = total[:, pl.ds(block * LANES, LANES)]
        out_ref[block, :NRHS, :] = terms[:NRHS] + terms[NRHS : 2 * NRHS] + terms[2 * NRHS :]


def parts_of(left_block, right_block):
    kernel = jnp.exp2(dot(left_block, right_block))
    high = kernel.astype(jnp.bfloat16)
    return high, (kernel - high.astype(jnp.float32)).astype(jnp.bfloat16)


def chunk_terms(left, right, vector, rows, span):
    high, low = parts_of(left[rows, :], right[:, span])
    return jnp.concatenate([dot(vector[:, rows], high), dot(vector[:NRHS, rows], low)], axis=0)


def multiply(value_of, out_ref, left, right, vector, total):
    split_vector(value_of, vector)
    for place in range(total.shape[1] // WIDE):
        span = pl.ds(place * WIDE, WIDE)
        terms = [chunk_terms(left, right, vector, pl.ds(begin, CHUNK), span) for begin in range(0, left.shape[0], CHUNK)]
        total[:, span] = functools.reduce(jnp.add, terms)
    write_terms(total, out_ref)


def first_kernel(left_ref, right_ref, out_ref, left, right, vector, total):
    write_right(right_ref, right)
    write_left(left_ref, left)
    multiply(lambda block: left_ref[block, NFEAT:, :], out_ref, left, right, vector, total)


def second_kernel(left_ref, image_ref, left, right, out_ref, vector, total):
    multiply(lambda block: image_ref[block], out_ref, left, right, vector, total)
    square = jnp.zeros((NRHS, LANES), jnp.float32)
    product = jnp.zeros((NRHS, LANES), jnp.float32)
    for block in range(left_ref.shape[0]):
        target = left_ref[block, NFEAT:, :]
        square += target * target
        product += target * image_ref[block]
    empty = jnp.zeros((LANES - 2 * NRHS, LANES), jnp.float32)
    turned = jnp.concatenate([square, product, empty], axis=0).T
    row = jnp.sum(turned, axis=0, keepdims=True)
    for block in range(out_ref.shape[0]):
        out_ref[block, NRHS:, :] = jnp.broadcast_to(row, (SUMS, LANES))


VMEM_BLOCK = pl.BlockSpec(memory_space=pltpu.VMEM)


def product_scratch(left_count, right_count):
    return [
        pltpu.VMEM((2 * NRHS, left_count), jnp.bfloat16),
        pltpu.VMEM((3 * NRHS, right_count), jnp.float32),
    ]


def first_terms(left, right):
    left_count, right_count = left.shape[0] * LANES, right.shape[0] * LANES
    return pl.pallas_call(
        first_kernel,
        out_shape=[
            jax.ShapeDtypeStruct((right.shape[0], NRHS, LANES), jnp.float32),
            jax.ShapeDtypeStruct((left_count, FEATURE_ROWS), jnp.bfloat16),
            jax.ShapeDtypeStruct((FEATURE_ROWS, right_count), jnp.bfloat16),
        ],
        in_specs=[VMEM_BLOCK] * 2,
        out_specs=[VMEM_BLOCK] * 3,
        scratch_shapes=product_scratch(left_count, right_count),
        compiler_params=pltpu.CompilerParams(vmem_limit_bytes=VMEM_LIMIT),
    )(left, right)


def second_terms(left, image, left_features, right_features):
    left_count, right_count = left_features.shape[0], right_features.shape[1]
    return pl.pallas_call(
        second_kernel,
        out_shape=jax.ShapeDtypeStruct((right_count // LANES, NRHS + SUMS, LANES), jnp.float32),
        in_specs=[VMEM_BLOCK] * 4,
        out_specs=VMEM_BLOCK,
        scratch_shapes=product_scratch(left_count, right_count),
        compiler_params=pltpu.CompilerParams(vmem_limit_bytes=VMEM_LIMIT),
    )(left, image, left_features, right_features)


def exchange(blocks, axis):
    return lax.all_to_all(blocks, axis, 0, 0, tiled=True)


def gather(block, axis, count):
    return exchange(jnp.broadcast_to(block[None], (count,) + block.shape), axis)


def row_of(sums):
    return jnp.pad(jnp.concatenate(sums), (0, LANES - NRHS * len(sums)))[None]


def inner(left, right):
    return jnp.sum(left * right, axis=1)


def on_device(rows, cols, points, inverse_scale, targets, noise_var):
    noise = noise_var[:, None]
    known = jnp.concatenate([points * inverse_scale[:, None], targets], axis=0)
    known = lax.optimization_barrier(known)
    targets = known[NFEAT:]
    left = gather(known, ROW, rows)
    right = lax.all_gather(known[:NFEAT], COL, axis=0)
    right, noise_terms = lax.optimization_barrier((right, noise * targets))

    partial, *kept = first_terms(left, right)
    image = jnp.sum(exchange(partial, COL), axis=0) + noise_terms
    partial = second_terms(left, gather(image, ROW, rows), *kept)
    reduced = jnp.sum(exchange(partial, COL), axis=0)
    image_image = reduced[:NRHS] + noise * image

    norm_now, curvature = reduced[NRHS, :NRHS], reduced[NRHS, NRHS : 2 * NRHS]
    step_size = (norm_now / curvature)[:, None]
    residual = targets - step_size * image
    residual_image = image - step_size * image_image
    sums = row_of([inner(residual, residual), inner(residual, residual_image), inner(residual, image)])
    sums = jnp.sum(gather(sums, COL, cols), axis=0)
    sums = jnp.sum(gather(sums, ROW, rows), axis=0)[0]
    norm_next = sums[:NRHS]
    ratio = norm_next / norm_now
    next_curvature = sums[NRHS : 2 * NRHS] + ratio * (2.0 * sums[2 * NRHS : 3 * NRHS] + ratio * curvature)
    next_step = (norm_next / next_curvature)[:, None]
    ratio = ratio[:, None]
    solution = step_size * targets + next_step * (residual + ratio * targets)
    residual = residual - next_step * (residual_image + ratio * image)
    return (solution, residual)


def size_of(mesh, axes):
    return math.prod(mesh.shape[axis] for axis in axes)


def solution(mesh):
    mesh = jax.sharding.Mesh(mesh.devices.reshape(SHAPE), AXES)
    return jax.shard_map(
        functools.partial(on_device, size_of(mesh, ROW), size_of(mesh, COL)),
        mesh=mesh,
        in_specs=(P(None, AXES), P(), P(None, AXES), P()),
        out_specs=(P(None, AXES), P(None, AXES)),
        check_vma=False,
    )
```
